32 devices in a mesh: wide: 8 (over y, x, core), node: 4 (over z).
Axes of the slice: x: 2, y: 2, z: 4, core: 2. Of those that a mesh axis runs over, the one named last changes fastest.
Arguments:
- normed: bfloat16 [16384, 4096], P(('wide', 'node')), may hold values from -6 to 6
- queries: bfloat16 [16384, 2048], P(('wide', 'node')), may hold values from -48 to 48
- keys: bfloat16 [16384, 512], P(('wide', 'node')), may hold values from -6 to 6
- values: bfloat16 [16384, 512], P(('wide', 'node')), may hold values from -6 to 6
- attn_grad: bfloat16 [16384, 2048], P(('wide', 'node')), may hold values from -6 to 6
- kv_proj: bfloat16 [4096, 1024], P(None, 'node'), may hold values from -0.09375 to 0.09375
Outputs:
- query_grad: bfloat16 [16384, 2048], P(('wide', 'node'))
- input_grad: bfloat16 [16384, 4096], P(('wide', 'node'))
- weight_grad: float32 [4096, 1024], P(('wide', 'node'))
The draws below stay inside these ranges and needn't reach their ends.
All inputs are finite; a program needn't handle non-finite values.
Results may differ from the reference program's by a relative error of at most 0.019.
Values may be sent and summed in bfloat16 or wider, within the bound.
A program may use at most 192 MiB of HBM per device.

```python
import jax
import jax.numpy as jnp
from jax import lax

D = 4096
HQ = 16
KVH = 4
HD = 128
TOK_DEV = 512
TOKENS = 16384


def draw_pair(key):
    key_base = jax.random.fold_in(key, 71)
    key_draw, query_draw = jax.random.split(key_base)
    key_vals = jnp.clip(jax.random.normal(key_draw, (TOKENS, KVH, HD), jnp.float32), -6.0, 6.0)
    query_vals = jnp.clip(jax.random.normal(query_draw, (TOKENS, KVH, HQ // KVH, HD), jnp.float32), -6.0, 6.0)
    return (query_vals.reshape(TOKENS, HQ * HD), key_vals.reshape(TOKENS, KVH * HD))


def draw_queries(key, part):
    return draw_pair(key)[0].astype(jnp.bfloat16)


def draw_keys(key, part):
    return draw_pair(key)[1].astype(jnp.bfloat16)


def with_spikes(drawn, key, source, target, shards_of, factor):
    owner, partner = [(jnp.arange(drawn.shape[dim]) // (drawn.shape[dim] // shards_of)).reshape([-1 if axis == dim else 1 for axis in range(drawn.ndim)]) for dim in (source, target)]
    chosen = jax.random.permutation(key, shards_of)[partner]
    strong = (owner == chosen) | (owner == (partner + shards_of // 2) % shards_of)
    return jnp.where(strong, factor * drawn, drawn)


def shard_levels(own_key, dims, cuts, low, top_value):
    loudness = 1.0
    for dim, parts in cuts:
        draws = jax.random.uniform(jax.random.fold_in(jax.random.fold_in(own_key, 6), dim), (parts,), jnp.float32, low / len(cuts), top_value / len(cuts))
        loudness = loudness * jnp.repeat(jnp.exp(draws), dims[dim] // parts).reshape((-1,) + (1,) * (len(dims) - 1 - dim))
    return loudness


def scatter_about(key, dims, scale, bound, cuts=(), kind=jnp.bfloat16):
    level = shard_levels(key, dims, cuts, -0.22, 0.18) if cuts else 1.0
    entries = jax.random.normal(key, dims, jnp.float32) * scale * level
    return jnp.minimum(jnp.maximum(entries, -bound), bound).astype(kind)


def heavy_noise(rng, shape, scale, bound, shards, heavy, kind=jnp.bfloat16):
    drawn = scale * jax.random.normal(rng, shape, jnp.float32)
    if shards:
        drawn = drawn * shard_levels(rng, shape, shards, -0.22, 0.18)
    return jnp.clip(with_spikes(drawn, jax.random.fold_in(rng, 3), *heavy), -bound, bound).astype(kind)


def setup_inputs(seed: int = 0) -> dict:
    arg_keys = jax.random.split(jax.random.key(seed), 7)
    normed = heavy_noise(arg_keys[0], (TOKENS, D), 1.0, 6.0, ((0, 32),), (0, 1, 32, 2.75))
    queries = draw_queries(jax.random.fold_in(arg_keys[6], 71), 0)
    keys = draw_keys(jax.random.fold_in(arg_keys[6], 71), 0)
    values = scatter_about(arg_keys[3], (TOKENS, KVH * HD), 1.0, 6.0, ((0, 32),))
    attn_grad = scatter_about(arg_keys[4], (TOKENS, HQ * HD), 1.0, 6.0, ((0, 32),))
    kv_proj = scatter_about(arg_keys[5], (D, 2 * KVH * HD), D ** -0.5, 0.09375, ((1, 4),))
    return {"normed": normed, "queries": queries, "keys": keys, "values": values, "attn_grad": attn_grad, "kv_proj": kv_proj}


ROPE_BASE = 500000.0


def rope_tables(length, size):
    half_size = size // 2
    frequency = jnp.power(jnp.float32(ROPE_BASE), -jnp.arange(half_size, dtype=jnp.float32) * (2.0 / size))
    angles = jnp.arange(length, dtype=jnp.float32)[:, None] * frequency[None, :]
    cosine = jnp.concatenate([jnp.cos(angles), jnp.cos(angles)], axis=1)
    sine_tab = jnp.concatenate([jnp.sin(angles), jnp.sin(angles)], axis=1)
    return cosine, sine_tab


def sequence_grads(queries, keys, values, attn_grad, cosine, sine_tab):
    length = queries.shape[0]
    query_heads = queries.reshape(length, KVH, HQ // KVH, HD).astype(jnp.float32)
    key_heads = keys.reshape(length, KVH, HD).astype(jnp.float32)
    value_heads = values.reshape(length, KVH, HD).astype(jnp.float32)
    grad_heads = attn_grad.reshape(length, KVH, HQ // KVH, HD).astype(jnp.float32)
    inv_root = HD ** -0.5
    scores = jnp.einsum("tkgd,skd->kgts", query_heads, key_heads) * inv_root
    positions = jnp.arange(length, dtype=jnp.int32)
    causal_mask = positions[:, None] >= positions[None, :]
    scores = jnp.where(causal_mask, scores, -jnp.inf)
    row_max = jnp.max(scores, axis=-1, keepdims=True)
    exponent = jnp.exp(scores - row_max)
    prob_full = exponent / jnp.sum(exponent, axis=-1, keepdims=True)
    prob_low = prob_full.astype(jnp.bfloat16)
    grad_prob = jnp.einsum("tkgd,skd->kgts", grad_heads, value_heads)
    row_delta = jnp.sum(prob_full * grad_prob, axis=-1, keepdims=True)
    grad_score = (prob_full * (grad_prob - row_delta) * inv_root).astype(jnp.bfloat16)
    grad_wide = grad_score.astype(jnp.float32)
    query_grad = jnp.einsum("kgts,skd->tkgd", grad_wide, key_heads).astype(jnp.bfloat16).reshape(length, HQ * HD)
    key_grad = jnp.einsum("kgts,tkgd->skd", grad_wide, query_heads)
    value_grad = jnp.einsum("kgts,tkgd->skd", prob_low.astype(jnp.float32), grad_heads).astype(jnp.bfloat16)
    half_size = HD // 2
    sine_part = key_grad * sine_tab[:, None, :]
    key_unrot = key_grad * cosine[:, None, :] + jnp.concatenate([sine_part[..., half_size:], -sine_part[..., :half_size]], axis=-1)
    kv_grad = jnp.concatenate([key_unrot.astype(jnp.bfloat16).reshape(length, KVH * HD), value_grad.reshape(length, KVH * HD)], axis=1)
    return query_grad, kv_grad


def reference(normed, queries, keys, values, attn_grad, kv_proj):
    seq_count = TOKENS // TOK_DEV
    cosine, sine_tab = rope_tables(TOK_DEV, HD)
    grad_scale = TOKENS ** -0.5

    def per_sequence(accum_grad, seq_index):
        offset = (seq_index * TOK_DEV).astype(jnp.int32)
        normed_seq = lax.dynamic_slice_in_dim(normed, offset, TOK_DEV, 0)
        query_seq = lax.dynamic_slice_in_dim(queries, offset, TOK_DEV, 0)
        key_seq = lax.dynamic_slice_in_dim(keys, offset, TOK_DEV, 0)
        value_seq = lax.dynamic_slice_in_dim(values, offset, TOK_DEV, 0)
        grad_seq = lax.dynamic_slice_in_dim(attn_grad, offset, TOK_DEV, 0)
        query_out, kv_grad = sequence_grads(query_seq, key_seq, value_seq, grad_seq, cosine, sine_tab)
        input_out = jnp.dot(kv_grad, kv_proj.T, preferred_element_type=jnp.float32).astype(jnp.bfloat16)
        accum_grad = accum_grad + jnp.dot(normed_seq.T, kv_grad, preferred_element_type=jnp.float32) * grad_scale
        return accum_grad, (query_out, input_out)

    start_grad = jnp.zeros((D, 2 * KVH * HD), jnp.float32)
    weight_grad, (query_out, input_out) = lax.scan(per_sequence, start_grad, jnp.arange(seq_count, dtype=jnp.int32))
    return query_out.reshape(TOKENS, HQ * HD), input_out.reshape(TOKENS, D), weight_grad
```

```python
import functools
import math

import jax
import jax.numpy as jnp
from jax import lax
from jax.experimental import pallas as pl
from jax.experimental.pallas import tpu as pltpu
from jax.sharding import PartitionSpec as P

HQ = 16
KVH = 4
HD = 128
GROUP = HQ // KVH
ROPE_BASE = 500000.0
MESH = pl.DeviceIdType.MESH
F32 = jnp.float32
BF16 = jnp.bfloat16


def rope_tables(length, size):
    half_size = size // 2
    frequency = jnp.power(F32(ROPE_BASE), -jnp.arange(half_size, dtype=F32) * (2.0 / size))
    angles = jnp.arange(length, dtype=F32)[:, None] * frequency[None, :]
    cosine = jnp.concatenate([jnp.cos(angles), jnp.cos(angles)], axis=1)
    sine = jnp.concatenate([jnp.sin(angles), -jnp.sin(angles)], axis=1)
    return cosine, sine


def dot(a, b, ca, cb):
    return lax.dot_general(a, b, (((ca,), (cb,)), ((), ())), preferred_element_type=F32)


def kernel(W, N, grad_scale, normed, queries, keys, values, attn_grad, kv_proj, cosine, sine,
           query_out, input_out, weight_out,
           q_v, g_v, k_v, v_v, cos_v, sin_v, kt_v, dk_v, dv_v, qg_v, nx, kvt, kvg, kvp,
           wsend, wrecv, nbuf, nrecv, ig_v, wo_v,
           qg_sem, kv_sem, nx_sem, own_sem, out_sem, ig_sem,
           nxs_s, nxs_r, kvs_s, kvs_r, pl_s, pl_r, nd_s, nd_r,
           agz_s, agz_r, agp_s, agp_r, ags_s, ags_r):
    T, D = normed.shape
    C = kvp.shape[1]
    KC = KVH * HD
    CB = kv_proj.shape[1]
    PC = W // 2
    R = D // (W * N)
    SN = N * R
    RW = D // W
    HB = GROUP * HD
    w = lax.axis_index("wide")
    n = lax.axis_index("node")
    core = lax.rem(w, 2)
    chip = lax.div(w, 2)
    sib = (chip * 2 + (1 - core), n)

    def chip_at(d):
        return lax.rem(chip + d, PC)

    def node_at(d):
        return lax.rem(n + d, N)

    def plane(d):
        return (chip_at(d) * 2 + core, n)

    def col(i, size):
        return pl.ds(pl.multiple_of(i * size, size), size)

    def remote(src, dst, s, r, dev):
        return pltpu.make_async_remote_copy(
            src_ref=src, dst_ref=dst, send_sem=s, recv_sem=r, device_id=dev, device_id_type=MESH)

    loads = [pltpu.make_async_copy(a, b, kv_sem.at[i]) for i, (a, b) in enumerate(
        ((keys, k_v), (values, v_v), (cosine, cos_v), (sine, sin_v)))]
    head_loads = []
    for k in range(KVH):
        c = pl.ds(k * HB, HB)
        head_loads.append((
            pltpu.make_async_copy(queries.at[:, c], q_v.at[:, c], qg_sem.at[0, k]),
            pltpu.make_async_copy(attn_grad.at[:, c], g_v.at[:, c], qg_sem.at[1, k])))
    for x in loads[:2] + list(head_loads[0]) + loads[2:]:
        x.start()
    for k in range(1, KVH):
        for x in head_loads[k]:
            x.start()
    nx_loads = [pltpu.make_async_copy(normed.at[:, col(p * 2 + core, SN)], nx.at[p, 0], nx_sem.at[p])
                for p in range(PC)]
    own = pltpu.make_async_copy(kv_proj, kvp.at[:, col(n, CB)], own_sem)

    barrier = pltpu.get_barrier_semaphore()
    partners = [sib] + [plane(d) for d in range(1, PC)] + [(w, node_at(d)) for d in range(1, N)]
    for dev in partners:
        pl.semaphore_signal(barrier, inc=1, device_id=dev, device_id_type=MESH)
    for x in nx_loads:
        x.start()
    own.start()
    pl.semaphore_wait(barrier, len(partners))

    rows_w = col(w, RW)
    agz = {d: remote(kv_proj.at[rows_w, :], kvp.at[rows_w, col(n, CB)],
                     agz_s.at[d], agz_r.at[d], (w, node_at(d))) for d in range(1, N)}
    for d in agz:
        agz[d].start()
    nxs = [remote(normed.at[:, col(p * 2 + 1 - core, SN)], nx.at[p, 1], nxs_s.at[p], nxs_r.at[p], sib)
           for p in range(PC)]
    for x in nxs:
        x.start()

    inv_root = HD ** (-0.5)
    c2 = inv_root * math.log2(math.e)
    TB = T // 2
    out_copies = []

    def attention(k):
        for x in head_loads[k]:
            x.wait()
        kc = pl.ds(k * HD, HD)
        kt_v[...] = k_v[:, kc].astype(F32).T.astype(BF16)
        dk_v[...] = jnp.zeros_like(dk_v)
        dv_v[...] = jnp.zeros_like(dv_v)

        def head(g, carry):
            hc = col(k * GROUP + g, HD)
            for j in range(2):
                L = (j + 1) * TB
                tr = pl.ds(j * TB, TB)
                q = q_v[tr, hc]
                do = g_v[tr, hc]
                s = dot(k_v[:L, kc], q, 1, 1)
                dp = dot(v_v[:L, kc], do, 1, 1)
                si = lax.broadcasted_iota(jnp.int32, (L, TB), 0)
                ti = lax.broadcasted_iota(jnp.int32, (L, TB), 1) + j * TB
                s = jnp.where(si <= ti, s, -jnp.inf)
                m = jnp.max(s, axis=0, keepdims=True)
                e = jnp.exp2((s - m) * c2)
                p = e * (1.0 / jnp.sum(e, axis=0, keepdims=True))
                delta = jnp.sum(p * dp, axis=0, keepdims=True)
                ds = (p * (dp - delta)).astype(BF16)
                dq = dot(kt_v[:, :L], ds, 1, 0) * inv_root
                qg_v[tr, hc] = dq.T.astype(BF16)
                dk_v[:L, :] += dot(ds, q, 1, 0)
                dv_v[:L, :] += dot(p.astype(BF16), do, 1, 0)
            return carry

        lax.fori_loop(0, GROUP, head, 0)
        kg = dk_v[...] * inv_root
        ku = kg * cos_v[...] + pltpu.roll(kg, HD // 2, 1) * sin_v[...]
        vg = dv_v[...]
        kvg[:, pl.ds(k * HD, HD)] = ku.astype(BF16)
        kvg[:, pl.ds(KC + k * HD, HD)] = vg.astype(BF16)
        kvt[k, 0, :HD, :] = ku.T.astype(BF16)
        kvt[k, 0, HD:, :] = vg.T.astype(BF16)
        c = pl.ds(k * HB, HB)
        oc = pltpu.make_async_copy(qg_v.at[:, c], query_out.at[:, c], out_sem.at[k])
        oc.start()
        out_copies.append(oc)
        x = remote(kvt.at[k, 0], kvt.at[k, 1], kvs_s.at[k], kvs_r.at[k], sib)
        x.start()
        return x

    def weight_part(k, kv_copy):
        kv_copy.wait_recv()
        copies = []
        for d in list(range(1, PC)) + [0]:
            p = chip_at(d)
            term = dot(kvt[k, 0], nx[p, 0], 1, 0) + dot(kvt[k, 1], nx[p, 1], 1, 0)
            wsend[k, d] = (term * grad_scale).astype(BF16)
            if d:
                x = remote(wsend.at[k, d], wrecv.at[k, d - 1], pl_s.at[k, d], pl_r.at[k, d], plane(d))
                x.start()
                copies.append(x)
        return copies

    def plane_sum(k, copies):
        for x in copies:
            x.wait_recv()
        total = wsend[k, 0].astype(F32)
        for d in range(1, PC):
            total += wrecv[k, d - 1].astype(F32)
        nbuf[k] = total.T.astype(BF16)
        sends = []
        for d in range(1, N):
            x = remote(nbuf.at[k, col(node_at(d), R), :], nrecv.at[k, d - 1], nd_s.at[k, d], nd_r.at[k, d],
                       (w, node_at(d)))
            x.start()
            sends.append(x)
        return sends

    def final_sum(k, copies):
        for x in copies:
            x.wait_recv()
        total = nbuf[k, col(n, R), :].astype(F32)
        for d in range(1, N):
            total += nrecv[k, d - 1].astype(F32)
        wo_v[:, pl.ds(k * HD, HD)] = total[:, :HD]
        wo_v[:, pl.ds(KC + k * HD, HD)] = total[:, HD:]

    def gather_plane():
        copies, direct = [], []
        for d in range(1, N):
            agz[d].wait_recv()
            blk = kvp.at[rows_w, col(node_at(N - d), CB)]
            for e in range(1, PC):
                x = remote(blk, blk, agp_s.at[d, e], agp_r.at[d, e], plane(e))
                x.start()
                copies.append((d, e, x))
            x = remote(blk, blk, ags_s.at[d, 0], ags_r.at[d, 0], sib)
            x.start()
            direct.append(x)
        return copies, direct

    def gather_sibling(copies):
        done = []
        for d, e, c in copies:
            c.wait_recv()
            blk = kvp.at[col(chip_at(PC - e) * 2 + core, RW), col(node_at(N - d), CB)]
            x = remote(blk, blk, ags_s.at[d, e], ags_r.at[d, e], sib)
            x.start()
            done.append(x)
        return done

    for x in loads:
        x.wait()
    kvc = [attention(0), attention(1)]
    for p in range(PC):
        nx_loads[p].wait()
        nxs[p].wait_recv()
    wc = [weight_part(0, kvc[0])]
    kvc.append(attention(2))
    wc.append(weight_part(1, kvc[1]))
    agp, ags = gather_plane()
    kvc.append(attention(3))
    wc.append(weight_part(2, kvc[2]))
    nc = [plane_sum(0, wc[0])]
    wc.append(weight_part(3, kvc[3]))
    nc.append(plane_sum(1, wc[1]))
    ags = ags + gather_sibling(agp)
    nc.append(plane_sum(2, wc[2]))
    nc.append(plane_sum(3, wc[3]))

    for x in ags:
        x.wait_recv()
    own.wait()
    OB = 512
    NB = D // OB

    def input_block(b, carry):
        oc = col(b, OB)
        ig_v[:, oc] = dot(kvg[...], kvp[oc, :], 1, 1).astype(BF16)
        pltpu.make_async_copy(ig_v.at[:, oc], input_out.at[:, oc], ig_sem.at[b]).start()
        return carry

    lax.fori_loop(0, NB, input_block, 0)
    for k in range(KVH):
        final_sum(k, nc[k])
    wcopy = pltpu.make_async_copy(wo_v, weight_out, out_sem.at[KVH])
    wcopy.start()

    for x in list(agz.values()) + nxs + kvc + [c for _, _, c in agp] + ags:
        x.wait_send()
    for group in wc + nc:
        for x in group:
            x.wait_send()
    for x in out_copies:
        x.wait()
    for b in range(NB):
        oc = pl.ds(b * OB, OB)
        pltpu.make_async_copy(ig_v.at[:, oc], input_out.at[:, oc], ig_sem.at[b]).wait()
    wcopy.wait()


def local(normed, queries, keys, values, attn_grad, kv_proj):
    T, D = normed.shape
    W = lax.axis_size("wide")
    N = lax.axis_size("node")
    C = 2 * KVH * HD
    CB = kv_proj.shape[1]
    PC = W // 2
    R = D // (W * N)
    SN = N * R
    cosine, sine = rope_tables(T, HD)
    grad_scale = (T * W * N) ** (-0.5)
    dma = pltpu.SemaphoreType.DMA
    any_spec = pl.BlockSpec(memory_space=pl.ANY)
    flops = 2 * T * (HQ * 5 * T * HD + 3 * D * C)
    return pl.pallas_call(
        functools.partial(kernel, W, N, grad_scale),
        out_shape=(
            jax.ShapeDtypeStruct((T, HQ * HD), BF16),
            jax.ShapeDtypeStruct((T, D), BF16),
            jax.ShapeDtypeStruct((R, C), F32),
        ),
        in_specs=[any_spec] * 8,
        out_specs=(any_spec,) * 3,
        scratch_shapes=[
            pltpu.VMEM((T, HQ * HD), BF16),
            pltpu.VMEM((T, HQ * HD), BF16),
            pltpu.VMEM((T, KVH * HD), BF16),
            pltpu.VMEM((T, KVH * HD), BF16),
            pltpu.VMEM((T, HD), F32),
            pltpu.VMEM((T, HD), F32),
            pltpu.VMEM((HD, T), BF16),
            pltpu.VMEM((T, HD), F32),
            pltpu.VMEM((T, HD), F32),
            pltpu.VMEM((T, HQ * HD), BF16),
            pltpu.VMEM((PC, 2, T, SN), BF16),
            pltpu.VMEM((KVH, 2, 2 * HD, T), BF16),
            pltpu.VMEM((T, C), BF16),
            pltpu.VMEM((D, C), BF16),
            pltpu.VMEM((KVH, PC, 2 * HD, SN), BF16),
            pltpu.VMEM((KVH, PC - 1, 2 * HD, SN), BF16),
            pltpu.VMEM((KVH, SN, 2 * HD), BF16),
            pltpu.VMEM((KVH, N - 1, R, 2 * HD), BF16),
            pltpu.VMEM((T, D), BF16),
            pltpu.VMEM((R, C), F32),
            dma((2, KVH)), dma((4,)), dma((PC,)), dma, dma((KVH + 1,)), dma((D // 512,)),
            dma((PC,)), dma((PC,)), dma((KVH,)), dma((KVH,)),
            dma((KVH, PC)), dma((KVH, PC)), dma((KVH, N)), dma((KVH, N)),
            dma((N,)), dma((N,)), dma((N, PC)), dma((N, PC)), dma((N, PC)), dma((N, PC)),
        ],
        compiler_params=pltpu.CompilerParams(
            collective_id=0, has_side_effects=True, vmem_limit_bytes=60 * 1024 * 1024),
        cost_estimate=pl.CostEstimate(flops=flops, bytes_accessed=24 * T * D, transcendentals=HQ * T * T),
    )(normed, queries, keys, values, attn_grad, kv_proj, cosine, sine)


def solution(mesh):
    rows = P(("wide", "node"), None)
    return jax.shard_map(
        local,
        mesh=mesh,
        in_specs=(rows, rows, rows, rows, rows, P(None, "node")),
        out_specs=(rows, rows, rows),
        check_vma=False,
    )
```

```python
import functools
import math

import jax
import jax.numpy as jnp
import numpy as np
from jax import lax
from jax.experimental import pallas as pl
from jax.experimental.pallas import tpu as pltpu
from jax.sharding import PartitionSpec as P

HQ = 16
KVH = 4
HD = 128
GROUP = HQ // KVH
ROPE_BASE = 500000.0
MESH = pl.DeviceIdType.MESH
F32 = jnp.float32
BF16 = jnp.bfloat16


def rope_tables(length, size):
    half_size = size // 2
    frequency = np.power(
        np.float32(ROPE_BASE), -np.arange(half_size, dtype=np.float32) * np.float32(2.0 / size)
    ).astype(np.float32)
    angles = np.arange(length, dtype=np.float32)[:, None] * frequency[None, :]
    cosine = np.cos(angles.astype(np.float64))
    sine = np.sin(angles.astype(np.float64))
    return (
        jnp.asarray(np.concatenate([cosine, cosine], axis=1), F32),
        jnp.asarray(np.concatenate([sine, -sine], axis=1), F32),
    )


def dot(a, b, ca, cb):
    return lax.dot_general(a, b, (((ca,), (cb,)), ((), ())), preferred_element_type=F32)


def plane_shape(W):
    chips = W // 2
    rows = 2 if chips % 2 == 0 else 1
    return rows, chips // rows


def kernel(W, N, grad_scale, normed, queries, keys, values, attn_grad, kv_proj, cosine, sine,
           query_out, input_out, weight_out,
           q_v, g_v, k_v, v_v, cos_v, sin_v, kt_v, dk_v, dv_v, qg_v, nx, kvt, kvg, kvp,
           wsend, wrecv, fsend, frecv, nbuf, nrecv, ig_v, wo_v,
           qg_sem, kv_sem, nx_sem, own_sem, out_sem, ig_sem,
           nxs_s, nxs_r, kvs_s, kvs_r, p1_s, p1_r, p2_s, p2_r, nd_s, nd_r,
           agz_s, agz_r, agp_s, agp_r, agf_s, agf_r, ags_s, ags_r):
    T, D = normed.shape
    C = kvp.shape[1]
    KC = KVH * HD
    CB = kv_proj.shape[1]
    PC = W // 2
    R = D // (W * N)
    SN = N * R
    SH = SN // 2
    RW = D // W
    A, B = plane_shape(W)
    HB = GROUP * HD
    w = lax.axis_index("wide")
    n = lax.axis_index("node")
    core = lax.rem(w, 2)
    chip = lax.div(w, 2)
    sib = (chip * 2 + (1 - core), n)

    ca, cb = lax.div(chip, B), lax.rem(chip, B)

    def chip_at(da, db):
        return lax.rem(ca + da, A) * B + lax.rem(cb + db, B)

    def node_at(d):
        return lax.rem(n + d, N)

    def plane(da, db):
        return (chip_at(da, db) * 2 + core, n)

    def col(i, size):
        return pl.ds(pl.multiple_of(i * size, size), size)

    def remote(src, dst, s, r, dev):
        return pltpu.make_async_remote_copy(
            src_ref=src, dst_ref=dst, send_sem=s, recv_sem=r, device_id=dev, device_id_type=MESH)

    loads = [pltpu.make_async_copy(a, b, kv_sem.at[i]) for i, (a, b) in enumerate(
        ((keys, k_v), (values, v_v), (cosine, cos_v), (sine, sin_v)))]
    head_loads = []
    for k in range(KVH):
        c = pl.ds(k * HB, HB)
        head_loads.append((
            pltpu.make_async_copy(queries.at[:, c], q_v.at[:, c], qg_sem.at[0, k]),
            pltpu.make_async_copy(attn_grad.at[:, c], g_v.at[:, c], qg_sem.at[1, k])))
    for x in loads[:2] + list(head_loads[0]) + loads[2:]:
        x.start()
    for k in range(1, KVH):
        for x in head_loads[k]:
            x.start()
    nx_loads = [pltpu.make_async_copy(normed.at[:, col(p * 2 + core, SN)], nx.at[p, 0], nx_sem.at[p])
                for p in range(PC)]
    own = pltpu.make_async_copy(kv_proj, kvp.at[:, col(n, CB)], own_sem)

    barrier = pltpu.get_barrier_semaphore()
    partners = [sib] + [plane(d, 0) for d in range(1, A)] + [plane(0, d) for d in range(1, B)] + [(w, node_at(d)) for d in range(1, N)]
    for dev in partners:
        pl.semaphore_signal(barrier, inc=1, device_id=dev, device_id_type=MESH)
    for x in nx_loads:
        x.start()
    own.start()
    pl.semaphore_wait(barrier, len(partners))

    rows_w = col(w, RW)
    agz = {d: remote(kv_proj.at[rows_w, :], kvp.at[rows_w, col(n, CB)],
                     agz_s.at[d], agz_r.at[d], (w, node_at(d))) for d in range(1, N)}
    for d in agz:
        agz[d].start()
    nxs = [remote(normed.at[:, col(p * 2 + 1 - core, SN)], nx.at[p, 1], nxs_s.at[p], nxs_r.at[p], sib)
           for p in range(PC)]
    for x in nxs:
        x.start()

    inv_root = HD ** (-0.5)
    c2 = inv_root * math.log2(math.e)
    TB = T // 2
    out_copies = []

    def attention(k):
        for x in head_loads[k]:
            x.wait()
        kc = pl.ds(k * HD, HD)
        kt_v[...] = k_v[:, kc].astype(F32).T.astype(BF16)
        dk_v[...] = jnp.zeros_like(dk_v)
        dv_v[...] = jnp.zeros_like(dv_v)

        def head(g, carry):
            hc = col(k * GROUP + g, HD)
            for j in range(2):
                L = (j + 1) * TB
                tr = pl.ds(j * TB, TB)
                q = q_v[tr, hc]
                do = g_v[tr, hc]
                s = dot(k_v[:L, kc], q, 1, 1)
                dp = dot(v_v[:L, kc], do, 1, 1)
                si = lax.broadcasted_iota(jnp.int32, (L, TB), 0)
                ti = lax.broadcasted_iota(jnp.int32, (L, TB), 1) + j * TB
                s = jnp.where(si <= ti, s, -jnp.inf)
                m = jnp.max(s, axis=0, keepdims=True)
                e = jnp.exp2((s - m) * c2)
                p = e * (1.0 / jnp.sum(e, axis=0, keepdims=True))
                delta = jnp.sum(p * dp, axis=0, keepdims=True)
                ds = (p * (dp - delta)).astype(BF16)
                dq = dot(kt_v[:, :L], ds, 1, 0) * inv_root
                qg_v[tr, hc] = dq.T.astype(BF16)
                dk_v[:L, :] += dot(ds, q, 1, 0)
                dv_v[:L, :] += dot(p.astype(BF16), do, 1, 0)
            return carry

        lax.fori_loop(0, GROUP, head, 0)
        kg = dk_v[...] * inv_root
        ku = kg * cos_v[...] + pltpu.roll(kg, HD // 2, 1) * sin_v[...]
        vg = dv_v[...]
        kvg[:, pl.ds(k * HD, HD)] = ku.astype(BF16)
        kvg[:, pl.ds(KC + k * HD, HD)] = vg.astype(BF16)
        kvt[k, 0, :HD, :] = ku.T.astype(BF16)
        kvt[k, 0, HD:, :] = vg.T.astype(BF16)
        c = pl.ds(k * HB, HB)
        oc = pltpu.make_async_copy(qg_v.at[:, c], query_out.at[:, c], out_sem.at[k])
        oc.start()
        out_copies.append(oc)
        x = remote(kvt.at[k, 0], kvt.at[k, 1], kvs_s.at[k], kvs_r.at[k], sib)
        x.start()
        return x

    sizes = ((B, A), (A, B))

    def offsets(h, d1, d2):
        return (d2, d1) if h == 0 else (d1, d2)

    def weight_part(k, kv_copy):
        kv_copy.wait_recv()
        copies = [[], []]

        def terms(h, d1):
            s2 = sizes[h][1]
            for d2 in range(s2):
                p = chip_at(*offsets(h, d1, d2))
                lanes = pl.ds(h * SH, SH)
                term = dot(kvt[k, 0], nx[p, 0, :, lanes], 1, 0) + dot(kvt[k, 1], nx[p, 1, :, lanes], 1, 0)
                wsend[k, h, d1 * s2 + d2] = (term * grad_scale).astype(BF16)
            if d1:
                x = remote(wsend.at[k, h, pl.ds(d1 * s2, s2)], wrecv.at[k, h, pl.ds((d1 - 1) * s2, s2)],
                           p1_s.at[k, h, d1], p1_r.at[k, h, d1], plane(*offsets(h, d1, 0)))
                x.start()
                copies[h].append(x)

        for d1 in range(1, max(A, B)):
            for h in range(2):
                if d1 < sizes[h][0]:
                    terms(h, d1)
        for h in range(2):
            terms(h, 0)
        return copies

    def first_total(k, h, d2):
        s1, s2 = sizes[h]
        total = wsend[k, h, d2].astype(F32)
        for d1 in range(1, s1):
            total += wrecv[k, h, (d1 - 1) * s2 + d2].astype(F32)
        return total

    def plane_first(k, copies):
        sends = [[], []]
        for h in range(2):
            for x in copies[h]:
                x.wait_recv()
            for d2 in range(1, sizes[h][1]):
                fsend[k, h, d2 - 1] = first_total(k, h, d2).astype(BF16)
                x = remote(fsend.at[k, h, d2 - 1], frecv.at[k, h, d2 - 1], p2_s.at[k, h, d2], p2_r.at[k, h, d2],
                           plane(*offsets(h, 0, d2)))
                x.start()
                sends[h].append(x)
        return sends

    def plane_second(k, copies):
        for h in range(2):
            total = first_total(k, h, 0)
            for x in copies[h]:
                x.wait_recv()
            for d2 in range(1, sizes[h][1]):
                total += frecv[k, h, d2 - 1].astype(F32)
            nbuf[k, pl.ds(h * SH, SH), :] = total.T.astype(BF16)
        sends = []
        for d in range(1, N):
            x = remote(nbuf.at[k, col(node_at(d), R), :], nrecv.at[k, d - 1], nd_s.at[k, d], nd_r.at[k, d],
                       (w, node_at(d)))
            x.start()
            sends.append(x)
        return sends

    def final_sum(k, copies):
        for x in copies:
            x.wait_recv()
        total = nbuf[k, col(n, R), :].astype(F32)
        for d in range(1, N):
            total += nrecv[k, d - 1].astype(F32)
        wo_v[:, pl.ds(k * HD, HD)] = total[:, :HD]
        wo_v[:, pl.ds(KC + k * HD, HD)] = total[:, HD:]

    RH = RW // 2

    def piece(d, da, db, half=None):
        first = (chip_at(A - da, B - db) * 2 + core) * RW
        rows = pl.ds(pl.multiple_of(first, RW), RW)
        if half is not None:
            rows = pl.ds(pl.multiple_of(first + half * RH, RH), RH)
        return kvp.at[rows, col(node_at(N - d), CB)]

    gathers = []

    def push(ref, s, r, dev):
        x = remote(ref, ref, s, r, dev)
        x.start()
        gathers.append(x)
        return x

    got = {}

    def gather_plane(d):
        agz[d].wait_recv()
        blk = piece(d, 0, 0)
        for db in range(1, B):
            got[d, 0, db] = [push(blk, agp_s.at[d, db], agp_r.at[d, db], plane(0, db))]
        for da in range(1, A):
            got[d, da, 0] = [push(blk, agp_s.at[d, da * B], agp_r.at[d, da * B], plane(da, 0))]
        got[d, 0, 0] = []
        to_sibling(d, 0, 0)

    def to_sibling(d, da, db):
        for x in got[d, da, db]:
            x.wait_recv()
        sibs[d, da, db] = push(piece(d, da, db), ags_s.at[d, da * B + db], ags_r.at[d, da * B + db], sib)

    sibs = {}

    def gather_forward(d):
        for da in range(1, A):
            for db in range(1, B):
                got[d, da, db] = []
        for db in range(1, B):
            to_sibling(d, 0, db)
            for da in range(1, A):
                i = da * B + db
                got[d, da, db].append(push(piece(d, 0, db, 0), agf_s.at[d, 0, i], agf_r.at[d, 0, i], plane(da, 0)))
        for da in range(1, A):
            to_sibling(d, da, 0)
            for db in range(1, B):
                i = da * B + db
                got[d, da, db].append(push(piece(d, da, 0, 1), agf_s.at[d, 1, i], agf_r.at[d, 1, i], plane(0, db)))

    def gather_last(d):
        for da in range(1, A):
            for db in range(1, B):
                to_sibling(d, da, db)

    for x in loads:
        x.wait()
    steps = [[], [], [], []]
    for d in range(1, N):
        steps[min(d - 1, 3)].append(d)

    def each(fn, i):
        for d in steps[i]:
            fn(d)

    OB = 512
    NB = D // OB

    def input_block(b, carry):
        oc = col(b, OB)
        ig_v[:, oc] = dot(kvg[...], kvp[oc, :], 1, 1).astype(BF16)
        pltpu.make_async_copy(ig_v.at[:, oc], input_out.at[:, oc], ig_sem.at[b]).start()
        return carry

    kvc = [attention(0), attention(1)]
    each(gather_plane, 0)
    for p in range(PC):
        nx_loads[p].wait()
        nxs[p].wait_recv()
    wc = [weight_part(0, kvc[0])]
    kvc.append(attention(2))
    each(gather_plane, 1)
    each(gather_forward, 0)
    wc.append(weight_part(1, kvc[1]))
    fc = [plane_first(0, wc[0])]
    kvc.append(attention(3))
    each(gather_plane, 2)
    each(gather_plane, 3)
    each(gather_forward, 1)
    wc.append(weight_part(2, kvc[2]))
    fc.append(plane_first(1, wc[1]))
    nc = [plane_second(0, fc[0])]
    each(gather_last, 0)
    wc.append(weight_part(3, kvc[3]))
    each(gather_forward, 2)
    each(gather_forward, 3)
    fc.append(plane_first(2, wc[2]))
    nc.append(plane_second(1, fc[1]))
    each(gather_last, 1)
    fc.append(plane_first(3, wc[3]))
    nc.append(plane_second(2, fc[2]))
    each(gather_last, 2)
    each(gather_last, 3)
    own.wait()
    for x in sibs.values():
        x.wait_recv()
    lax.fori_loop(0, NB // 2, input_block, 0)
    nc.append(plane_second(3, fc[3]))
    lax.fori_loop(NB // 2, NB, input_block, 0)
    for k in range(KVH):
        final_sum(k, nc[k])
    wcopy = pltpu.make_async_copy(wo_v, weight_out, out_sem.at[KVH])
    wcopy.start()

    for x in list(agz.values()) + nxs + kvc + gathers:
        x.wait_send()
    for halves in wc + fc:
        for x in halves[0] + halves[1]:
            x.wait_send()
    for group in nc:
        for x in group:
            x.wait_send()
    for x in out_copies:
        x.wait()
    for b in range(NB):
        oc = pl.ds(b * OB, OB)
        pltpu.make_async_copy(ig_v.at[:, oc], input_out.at[:, oc], ig_sem.at[b]).wait()
    wcopy.wait()


def local(normed, queries, keys, values, attn_grad, kv_proj):
    T, D = normed.shape
    W = lax.axis_size("wide")
    N = lax.axis_size("node")
    C = 2 * KVH * HD
    CB = kv_proj.shape[1]
    PC = W // 2
    R = D // (W * N)
    SN = N * R
    far = max(plane_shape(W))
    cosine, sine = rope_tables(T, HD)
    grad_scale = (T * W * N) ** (-0.5)
    dma = pltpu.SemaphoreType.DMA
    any_spec = pl.BlockSpec(memory_space=pl.ANY)
    flops = 2 * T * (HQ * 5 * T * HD + 3 * D * C)
    return pl.pallas_call(
        functools.partial(kernel, W, N, grad_scale),
        out_shape=(
            jax.ShapeDtypeStruct((T, HQ * HD), BF16),
            jax.ShapeDtypeStruct((T, D), BF16),
            jax.ShapeDtypeStruct((R, C), F32),
        ),
        in_specs=[any_spec] * 8,
        out_specs=(any_spec,) * 3,
        scratch_shapes=[
            pltpu.VMEM((T, HQ * HD), BF16),
            pltpu.VMEM((T, HQ * HD), BF16),
            pltpu.VMEM((T, KVH * HD), BF16),
            pltpu.VMEM((T, KVH * HD), BF16),
            pltpu.VMEM((T, HD), F32),
            pltpu.VMEM((T, HD), F32),
            pltpu.VMEM((HD, T), BF16),
            pltpu.VMEM((T, HD), F32),
            pltpu.VMEM((T, HD), F32),
            pltpu.VMEM((T, HQ * HD), BF16),
            pltpu.VMEM((PC, 2, T, SN), BF16),
            pltpu.VMEM((KVH, 2, 2 * HD, T), BF16),
            pltpu.VMEM((T, C), BF16),
            pltpu.VMEM((D, C), BF16),
            pltpu.VMEM((KVH, 2, PC, 2 * HD, SN // 2), BF16),
            pltpu.VMEM((KVH, 2, PC, 2 * HD, SN // 2), BF16),
            pltpu.VMEM((KVH, 2, far, 2 * HD, SN // 2), BF16),
            pltpu.VMEM((KVH, 2, far, 2 * HD, SN // 2), BF16),
            pltpu.VMEM((KVH, SN, 2 * HD), BF16),
            pltpu.VMEM((KVH, N - 1, R, 2 * HD), BF16),
            pltpu.VMEM((T, D), BF16),
            pltpu.VMEM((R, C), F32),
            dma((2, KVH)), dma((4,)), dma((PC,)), dma, dma((KVH + 1,)), dma((D // 512,)),
            dma((PC,)), dma((PC,)), dma((KVH,)), dma((KVH,)),
            dma((KVH, 2, far)), dma((KVH, 2, far)), dma((KVH, 2, far)), dma((KVH, 2, far)),
            dma((KVH, N)), dma((KVH, N)),
            dma((N,)), dma((N,)), dma((N, PC)), dma((N, PC)),
            dma((N, 2, PC)), dma((N, 2, PC)), dma((N, PC)), dma((N, PC)),
        ],
        compiler_params=pltpu.CompilerParams(
            collective_id=0, has_side_effects=True, vmem_limit_bytes=60 * 1024 * 1024),
        cost_estimate=pl.CostEstimate(flops=flops, bytes_accessed=24 * T * D, transcendentals=HQ * T * T),
    )(normed, queries, keys, values, attn_grad, kv_proj, cosine, sine)


def solution(mesh):
    rows = P(("wide", "node"), None)
    return jax.shard_map(
        local,
        mesh=mesh,
        in_specs=(rows, rows, rows, rows, rows, P(None, "node")),
        out_specs=(rows, rows, rows),
        check_vma=False,
    )
```

```python
import functools
import math

import jax
import jax.numpy as jnp
import numpy as np
from jax import lax
from jax.experimental import pallas as pl
from jax.experimental.pallas import tpu as pltpu
from jax.sharding import PartitionSpec as P

HQ = 16
KVH = 4
HD = 128
GROUP = HQ // KVH
ROPE_BASE = 500000.0
MESH = pl.DeviceIdType.MESH
F32 = jnp.float32
BF16 = jnp.bfloat16


def rope_tables(length, size):
    half_size = size // 2
    frequency = np.power(
        np.float32(ROPE_BASE), -np.arange(half_size, dtype=np.float32) * np.float32(2.0 / size)
    ).astype(np.float32)
    angles = np.arange(length, dtype=np.float32)[:, None] * frequency[None, :]
    cosine = np.cos(angles.astype(np.float64))
    sine = np.sin(angles.astype(np.float64))
    return (
        jnp.asarray(np.concatenate([cosine, cosine], axis=1), F32),
        jnp.asarray(np.concatenate([sine, -sine], axis=1), F32),
    )


def dot(a, b, ca, cb):
    return lax.dot_general(a, b, (((ca,), (cb,)), ((), ())), preferred_element_type=F32)


def plane_shape(W):
    chips = W // 2
    rows = 2 if chips % 2 == 0 else 1
    return rows, chips // rows


def kernel(W, N, grad_scale, normed, queries, keys, values, attn_grad, kv_proj, cosine, sine,
           query_out, input_out, weight_out,
           q_v, g_v, k_v, v_v, cos_v, sin_v, kt_v, dk_v, dv_v, qg_v, nx, kvt, kvg, kvp,
           wsend, wrecv, fsend, frecv, nbuf, nrecv, ig_v, wo_v,
           qg_sem, kv_sem, nx_sem, own_sem, out_sem, ig_sem,
           nxs_s, nxs_r, kvs_s, kvs_r, p1_s, p1_r, p2_s, p2_r, nd_s, nd_r,
           agz_s, agz_r, agp_s, agp_r, agf_s, agf_r, ags_s, ags_r):
    T, D = normed.shape
    C = kvp.shape[1]
    KC = KVH * HD
    CB = kv_proj.shape[1]
    PC = W // 2
    R = D // (W * N)
    SN = N * R
    SH = SN // 2
    RW = D // W
    A, B = plane_shape(W)
    HB = GROUP * HD
    w = lax.axis_index("wide")
    n = lax.axis_index("node")
    core = lax.rem(w, 2)
    chip = lax.div(w, 2)
    sib = (chip * 2 + (1 - core), n)

    ca, cb = lax.div(chip, B), lax.rem(chip, B)

    def chip_at(da, db):
        return lax.rem(ca + da, A) * B + lax.rem(cb + db, B)

    def node_at(d):
        return lax.rem(n + d, N)

    def plane(da, db):
        return (chip_at(da, db) * 2 + core, n)

    def col(i, size):
        return pl.ds(pl.multiple_of(i * size, size), size)

    def remote(src, dst, s, r, dev):
        return pltpu.make_async_remote_copy(
            src_ref=src, dst_ref=dst, send_sem=s, recv_sem=r, device_id=dev, device_id_type=MESH)

    loads = [pltpu.make_async_copy(a, b, kv_sem.at[i]) for i, (a, b) in enumerate(
        ((keys, k_v), (values, v_v), (cosine, cos_v), (sine, sin_v)))]
    head_loads = []
    for k in range(KVH):
        c = pl.ds(k * HB, HB)
        head_loads.append((
            pltpu.make_async_copy(queries.at[:, c], q_v.at[:, c], qg_sem.at[0, k]),
            pltpu.make_async_copy(attn_grad.at[:, c], g_v.at[:, c], qg_sem.at[1, k])))
    for x in loads[:2] + list(head_loads[0]) + loads[2:]:
        x.start()
    for k in range(1, KVH):
        for x in head_loads[k]:
            x.start()
    nx_loads = [pltpu.make_async_copy(normed.at[:, col(p * 2 + core, SN)], nx.at[p, 0], nx_sem.at[p])
                for p in range(PC)]
    own = pltpu.make_async_copy(kv_proj, kvp.at[:, col(n, CB)], own_sem)

    barrier = pltpu.get_barrier_semaphore()
    partners = [sib] + [plane(d, 0) for d in range(1, A)] + [plane(0, d) for d in range(1, B)] + [(w, node_at(d)) for d in range(1, N)]
    for dev in partners:
        pl.semaphore_signal(barrier, inc=1, device_id=dev, device_id_type=MESH)
    for x in nx_loads:
        x.start()
    own.start()
    pl.semaphore_wait(barrier, len(partners))

    rows_w = col(w, RW)
    agz = {d: remote(kv_proj.at[rows_w, :], kvp.at[rows_w, col(n, CB)],
                     agz_s.at[d], agz_r.at[d], (w, node_at(d))) for d in range(1, N)}
    near = [d for d in (1, N - 1) if 0 < d < N]
    order = list(dict.fromkeys(near + list(range(1, N))))
    for d in order:
        agz[d].start()
    nxs = [remote(normed.at[:, col(p * 2 + 1 - core, SN)], nx.at[p, 1], nxs_s.at[p], nxs_r.at[p], sib)
           for p in range(PC)]
    for x in nxs:
        x.start()

    inv_root = HD ** (-0.5)
    c2 = inv_root * math.log2(math.e)
    TB = T // 2
    out_copies = []

    def attention(k):
        for x in head_loads[k]:
            x.wait()
        kc = pl.ds(k * HD, HD)
        kt_v[...] = k_v[:, kc].astype(F32).T.astype(BF16)
        dk_v[...] = jnp.zeros_like(dk_v)
        dv_v[...] = jnp.zeros_like(dv_v)

        def head(g, carry):
            hc = col(k * GROUP + g, HD)
            q = q_v[:, hc]
            do = g_v[:, hc]
            scores, probs = [], []
            for j in range(2):
                L = (j + 1) * TB
                tr = slice(j * TB, (j + 1) * TB)
                s = dot(k_v[:L, kc], q[tr], 1, 1)
                dp = dot(v_v[:L, kc], do[tr], 1, 1)
                si = lax.broadcasted_iota(jnp.int32, (TB, TB), 0)
                ti = lax.broadcasted_iota(jnp.int32, (TB, TB), 1)
                last = jnp.where(si <= ti, s[L - TB:], -jnp.inf)
                s = jnp.concatenate([s[:L - TB], last], axis=0) if j else last
                m = jnp.max(s, axis=0, keepdims=True)
                e = jnp.exp2((s - m) * c2)
                p = e * (1.0 / jnp.sum(e, axis=0, keepdims=True))
                delta = jnp.sum(p * dp, axis=0, keepdims=True)
                ds = (p * (dp - delta)).astype(BF16)
                dq = dot(kt_v[:, :L], ds, 1, 0) * inv_root
                qg_v[pl.ds(j * TB, TB), hc] = dq.T.astype(BF16)
                scores.append(ds)
                probs.append(p.astype(BF16))
            for low, x, acc in ((scores, q, dk_v), (probs, do, dv_v)):
                acc[:TB, :] += dot(jnp.concatenate([low[0], low[1][:TB]], axis=1), x, 1, 0)
                acc[TB:, :] += dot(low[1][TB:], x[TB:], 1, 0)
            return carry

        lax.fori_loop(0, GROUP, head, 0, unroll=2)
        kg = dk_v[...] * inv_root
        ku = kg * cos_v[...] + pltpu.roll(kg, HD // 2, 1) * sin_v[...]
        vg = dv_v[...]
        kvg[:, pl.ds(k * HD, HD)] = ku.astype(BF16)
        kvg[:, pl.ds(KC + k * HD, HD)] = vg.astype(BF16)
        kvt[k, 0, :HD, :] = ku.T.astype(BF16)
        kvt[k, 0, HD:, :] = vg.T.astype(BF16)
        c = pl.ds(k * HB, HB)
        oc = pltpu.make_async_copy(qg_v.at[:, c], query_out.at[:, c], out_sem.at[k])
        oc.start()
        out_copies.append(oc)
        x = remote(kvt.at[k, 0], kvt.at[k, 1], kvs_s.at[k], kvs_r.at[k], sib)
        x.start()
        return x

    sizes = ((B, A), (A, B))

    def offsets(h, d1, d2):
        return (d2, d1) if h == 0 else (d1, d2)

    def weight_part(k, kv_copy):
        kv_copy.wait_recv()
        copies = [[], []]

        def terms(h, d1):
            s2 = sizes[h][1]
            for d2 in range(s2):
                p = chip_at(*offsets(h, d1, d2))
                lanes = pl.ds(h * SH, SH)
                term = dot(kvt[k, 0], nx[p, 0, :, lanes], 1, 0) + dot(kvt[k, 1], nx[p, 1, :, lanes], 1, 0)
                wsend[k, h, d1 * s2 + d2] = (term * grad_scale).astype(BF16)
            if d1:
                x = remote(wsend.at[k, h, pl.ds(d1 * s2, s2)], wrecv.at[k, h, pl.ds((d1 - 1) * s2, s2)],
                           p1_s.at[k, h, d1], p1_r.at[k, h, d1], plane(*offsets(h, d1, 0)))
                x.start()
                copies[h].append(x)

        for d1 in range(1, max(A, B)):
            for h in range(2):
                if d1 < sizes[h][0]:
                    terms(h, d1)
        for h in range(2):
            terms(h, 0)
        return copies

    def first_total(k, h, d2):
        s1, s2 = sizes[h]
        total = wsend[k, h, d2].astype(F32)
        for d1 in range(1, s1):
            total += wrecv[k, h, (d1 - 1) * s2 + d2].astype(F32)
        return total

    def plane_first(k, copies):
        sends = [[], []]
        for h in range(2):
            for x in copies[h]:
                x.wait_recv()
            for d2 in range(1, sizes[h][1]):
                fsend[k, h, d2 - 1] = first_total(k, h, d2).astype(BF16)
                x = remote(fsend.at[k, h, d2 - 1], frecv.at[k, h, d2 - 1], p2_s.at[k, h, d2], p2_r.at[k, h, d2],
                           plane(*offsets(h, 0, d2)))
                x.start()
                sends[h].append(x)
        return sends

    def plane_second(k, copies):
        for h in range(2):
            total = first_total(k, h, 0)
            for x in copies[h]:
                x.wait_recv()
            for d2 in range(1, sizes[h][1]):
                total += frecv[k, h, d2 - 1].astype(F32)
            nbuf[k, pl.ds(h * SH, SH), :] = total.T.astype(BF16)
        sends = []
        for d in range(1, N):
            x = remote(nbuf.at[k, col(node_at(d), R), :], nrecv.at[k, d - 1], nd_s.at[k, d], nd_r.at[k, d],
                       (w, node_at(d)))
            x.start()
            sends.append(x)
        return sends

    def final_sum(k, copies):
        for x in copies:
            x.wait_recv()
        total = nbuf[k, col(n, R), :].astype(F32)
        for d in range(1, N):
            total += nrecv[k, d - 1].astype(F32)
        wo_v[:, pl.ds(k * HD, HD)] = total[:, :HD]
        wo_v[:, pl.ds(KC + k * HD, HD)] = total[:, HD:]

    RH = RW // 2

    def piece(d, da, db, half=None):
        first = (chip_at(A - da, B - db) * 2 + core) * RW
        rows = pl.ds(pl.multiple_of(first, RW), RW)
        if half is not None:
            rows = pl.ds(pl.multiple_of(first + half * RH, RH), RH)
        return kvp.at[rows, col(node_at(N - d), CB)]

    gathers = []

    def push(ref, s, r, dev):
        x = remote(ref, ref, s, r, dev)
        x.start()
        gathers.append(x)
        return x

    got = {}

    def gather_plane(d):
        agz[d].wait_recv()
        blk = piece(d, 0, 0)
        for db in range(1, B):
            got[d, 0, db] = [push(blk, agp_s.at[d, db], agp_r.at[d, db], plane(0, db))]
        for da in range(1, A):
            got[d, da, 0] = [push(blk, agp_s.at[d, da * B], agp_r.at[d, da * B], plane(da, 0))]
        got[d, 0, 0] = []
        to_sibling(d, 0, 0)

    def to_sibling(d, da, db):
        for x in got[d, da, db]:
            x.wait_recv()
        sibs[d, da, db] = push(piece(d, da, db), ags_s.at[d, da * B + db], ags_r.at[d, da * B + db], sib)

    sibs = {}

    def gather_forward(d):
        for da in range(1, A):
            for db in range(1, B):
                got[d, da, db] = []
        for db in range(1, B):
            to_sibling(d, 0, db)
            for da in range(1, A):
                i = da * B + db
                got[d, da, db].append(push(piece(d, 0, db, 0), agf_s.at[d, 0, i], agf_r.at[d, 0, i], plane(da, 0)))
        for da in range(1, A):
            to_sibling(d, da, 0)
            for db in range(1, B):
                i = da * B + db
                got[d, da, db].append(push(piece(d, da, 0, 1), agf_s.at[d, 1, i], agf_r.at[d, 1, i], plane(0, db)))

    def gather_last(d):
        for da in range(1, A):
            for db in range(1, B):
                to_sibling(d, da, db)

    for x in loads:
        x.wait()
    steps = [order[:1], order[1:2], order[2:]]

    def each(fn, i):
        for d in steps[i]:
            fn(d)

    OB = 512
    NB = D // OB

    def input_block(b, carry):
        oc = col(b, OB)
        ig_v[:, oc] = dot(kvg[...], kvp[oc, :], 1, 1).astype(BF16)
        pltpu.make_async_copy(ig_v.at[:, oc], input_out.at[:, oc], ig_sem.at[b]).start()
        return carry

    kvc = [attention(0)]
    each(gather_plane, 0)
    for p in range(PC):
        nx_loads[p].wait()
        nxs[p].wait_recv()
    wc = [weight_part(0, kvc[0])]
    kvc.append(attention(1))
    each(gather_plane, 1)
    each(gather_forward, 0)
    wc.append(weight_part(1, kvc[1]))
    fc = [plane_first(0, wc[0])]
    kvc.append(attention(2))
    each(gather_plane, 2)
    each(gather_forward, 1)
    wc.append(weight_part(2, kvc[2]))
    fc.append(plane_first(1, wc[1]))
    nc = [plane_second(0, fc[0])]
    each(gather_last, 0)
    kvc.append(attention(3))
    each(gather_forward, 2)
    wc.append(weight_part(3, kvc[3]))
    fc.append(plane_first(2, wc[2]))
    nc.append(plane_second(1, fc[1]))
    each(gather_last, 1)
    each(gather_last, 2)
    own.wait()
    for x in sibs.values():
        x.wait_recv()
    lax.fori_loop(0, NB // 2, input_block, 0)
    fc.append(plane_first(3, wc[3]))
    nc.append(plane_second(2, fc[2]))
    lax.fori_loop(NB // 2, 3 * NB // 4, input_block, 0)
    nc.append(plane_second(3, fc[3]))
    lax.fori_loop(3 * NB // 4, NB, input_block, 0)
    for k in range(KVH):
        final_sum(k, nc[k])
    wcopy = pltpu.make_async_copy(wo_v, weight_out, out_sem.at[KVH])
    wcopy.start()

    for x in list(agz.values()) + nxs + kvc + gathers:
        x.wait_send()
    for halves in wc + fc:
        for x in halves[0] + halves[1]:
            x.wait_send()
    for group in nc:
        for x in group:
            x.wait_send()
    for x in out_copies:
        x.wait()
    for b in range(NB):
        oc = pl.ds(b * OB, OB)
        pltpu.make_async_copy(ig_v.at[:, oc], input_out.at[:, oc], ig_sem.at[b]).wait()
    wcopy.wait()


def local(normed, queries, keys, values, attn_grad, kv_proj):
    T, D = normed.shape
    W = lax.axis_size("wide")
    N = lax.axis_size("node")
    C = 2 * KVH * HD
    CB = kv_proj.shape[1]
    PC = W // 2
    R = D // (W * N)
    SN = N * R
    far = max(plane_shape(W))
    cosine, sine = rope_tables(T, HD)
    grad_scale = (T * W * N) ** (-0.5)
    dma = pltpu.SemaphoreType.DMA
    any_spec = pl.BlockSpec(memory_space=pl.ANY)
    flops = 2 * T * (HQ * 5 * T * HD + 3 * D * C)
    return pl.pallas_call(
        functools.partial(kernel, W, N, grad_scale),
        out_shape=(
            jax.ShapeDtypeStruct((T, HQ * HD), BF16),
            jax.ShapeDtypeStruct((T, D), BF16),
            jax.ShapeDtypeStruct((R, C), F32),
        ),
        in_specs=[any_spec] * 8,
        out_specs=(any_spec,) * 3,
        scratch_shapes=[
            pltpu.VMEM((T, HQ * HD), BF16),
            pltpu.VMEM((T, HQ * HD), BF16),
            pltpu.VMEM((T, KVH * HD), BF16),
            pltpu.VMEM((T, KVH * HD), BF16),
            pltpu.VMEM((T, HD), F32),
            pltpu.VMEM((T, HD), F32),
            pltpu.VMEM((HD, T), BF16),
            pltpu.VMEM((T, HD), F32),
            pltpu.VMEM((T, HD), F32),
            pltpu.VMEM((T, HQ * HD), BF16),
            pltpu.VMEM((PC, 2, T, SN), BF16),
            pltpu.VMEM((KVH, 2, 2 * HD, T), BF16),
            pltpu.VMEM((T, C), BF16),
            pltpu.VMEM((D, C), BF16),
            pltpu.VMEM((KVH, 2, PC, 2 * HD, SN // 2), BF16),
            pltpu.VMEM((KVH, 2, PC, 2 * HD, SN // 2), BF16),
            pltpu.VMEM((KVH, 2, far, 2 * HD, SN // 2), BF16),
            pltpu.VMEM((KVH, 2, far, 2 * HD, SN // 2), BF16),
            pltpu.VMEM((KVH, SN, 2 * HD), BF16),
            pltpu.VMEM((KVH, N - 1, R, 2 * HD), BF16),
            pltpu.VMEM((T, D), BF16),
            pltpu.VMEM((R, C), F32),
            dma((2, KVH)), dma((4,)), dma((PC,)), dma, dma((KVH + 1,)), dma((D // 512,)),
            dma((PC,)), dma((PC,)), dma((KVH,)), dma((KVH,)),
            dma((KVH, 2, far)), dma((KVH, 2, far)), dma((KVH, 2, far)), dma((KVH, 2, far)),
            dma((KVH, N)), dma((KVH, N)),
            dma((N,)), dma((N,)), dma((N, PC)), dma((N, PC)),
            dma((N, 2, PC)), dma((N, 2, PC)), dma((N, PC)), dma((N, PC)),
        ],
        compiler_params=pltpu.CompilerParams(
            collective_id=0, has_side_effects=True, vmem_limit_bytes=60 * 1024 * 1024),
        cost_estimate=pl.CostEstimate(flops=flops, bytes_accessed=24 * T * D, transcendentals=HQ * T * T),
    )(normed, queries, keys, values, attn_grad, kv_proj, cosine, sine)


def solution(mesh):
    rows = P(("wide", "node"), None)
    return jax.shard_map(
        local,
        mesh=mesh,
        in_specs=(rows, rows, rows, rows, rows, P(None, "node")),
        out_specs=(rows, rows, rows),
        check_vma=False,
    )
```

```python
import functools
import math

import jax
import jax.numpy as jnp
import numpy as np
from jax import lax
from jax.experimental import pallas as pl
from jax.experimental.pallas import tpu as pltpu
from jax.sharding import PartitionSpec as P

HQ = 16
KVH = 4
HD = 128
GROUP = HQ // KVH
ROPE_BASE = 500000.0
MESH = pl.DeviceIdType.MESH
F32 = jnp.float32
BF16 = jnp.bfloat16


def rope_tables(length, size):
    half_size = size // 2
    frequency = np.power(
        np.float32(ROPE_BASE), -np.arange(half_size, dtype=np.float32) * np.float32(2.0 / size)
    ).astype(np.float32)
    angles = np.arange(length, dtype=np.float32)[:, None] * frequency[None, :]
    cosine = np.cos(angles.astype(np.float64))
    sine = np.sin(angles.astype(np.float64))
    return (
        jnp.asarray(np.concatenate([cosine, cosine], axis=1), F32),
        jnp.asarray(np.concatenate([sine, -sine], axis=1), F32),
    )


def dot(a, b, ca, cb):
    return lax.dot_general(a, b, (((ca,), (cb,)), ((), ())), preferred_element_type=F32)


def plane_shape(W):
    chips = W // 2
    rows = 2 if chips % 2 == 0 else 1
    return rows, chips // rows


def kernel(W, N, grad_scale, normed, queries, keys, values, attn_grad, kv_proj, cosine, sine,
           query_out, input_out, weight_out,
           q_v, g_v, k_v, v_v, cos_v, sin_v, kt_v, dk_v, dv_v, qg_v, nx, kvt, kvg, kvp,
           wsend, wrecv, fsend, frecv, nbuf, nrecv, ig_v, wo_v,
           qg_sem, kv_sem, nx_sem, own_sem, out_sem, ig_sem,
           nxs_s, nxs_r, kvs_s, kvs_r, p1_s, p1_r, p2_s, p2_r, nd_s, nd_r,
           agz_s, agz_r, agp_s, agp_r, agf_s, agf_r, ags_s, ags_r):
    T, D = normed.shape
    C = kvp.shape[1]
    KC = KVH * HD
    CB = kv_proj.shape[1]
    PC = W // 2
    R = D // (W * N)
    SN = N * R
    SH = SN // 2
    RW = D // W
    A, B = plane_shape(W)
    HB = GROUP * HD
    w = lax.axis_index("wide")
    n = lax.axis_index("node")
    core = lax.rem(w, 2)
    chip = lax.div(w, 2)
    sib = (chip * 2 + (1 - core), n)

    ca, cb = lax.div(chip, B), lax.rem(chip, B)

    def chip_at(da, db):
        return lax.rem(ca + da, A) * B + lax.rem(cb + db, B)

    def node_at(d):
        return lax.rem(n + d, N)

    def plane(da, db):
        return (chip_at(da, db) * 2 + core, n)

    def col(i, size):
        return pl.ds(pl.multiple_of(i * size, size), size)

    def remote(src, dst, s, r, dev):
        return pltpu.make_async_remote_copy(
            src_ref=src, dst_ref=dst, send_sem=s, recv_sem=r, device_id=dev, device_id_type=MESH)

    loads = [pltpu.make_async_copy(a, b, kv_sem.at[i]) for i, (a, b) in enumerate(
        ((keys, k_v), (values, v_v), (cosine, cos_v), (sine, sin_v)))]
    head_loads = []
    for k in range(KVH):
        c = pl.ds(k * HB, HB)
        head_loads.append((
            pltpu.make_async_copy(queries.at[:, c], q_v.at[:, c], qg_sem.at[0, k]),
            pltpu.make_async_copy(attn_grad.at[:, c], g_v.at[:, c], qg_sem.at[1, k])))
    for x in loads[:2] + list(head_loads[0]) + loads[2:]:
        x.start()
    for k in range(1, KVH):
        for x in head_loads[k]:
            x.start()
    nx_loads = [pltpu.make_async_copy(normed.at[:, col(p * 2 + core, SN)], nx.at[p, 0], nx_sem.at[p])
                for p in range(PC)]
    own = pltpu.make_async_copy(kv_proj, kvp.at[:, col(n, CB)], own_sem)

    barrier = pltpu.get_barrier_semaphore()
    partners = [sib] + [plane(d, 0) for d in range(1, A)] + [plane(0, d) for d in range(1, B)] + [(w, node_at(d)) for d in range(1, N)]
    for dev in partners:
        pl.semaphore_signal(barrier, inc=1, device_id=dev, device_id_type=MESH)
    for x in nx_loads:
        x.start()
    own.start()
    pl.semaphore_wait(barrier, len(partners))

    rows_w = col(w, RW)
    agz = {d: remote(kv_proj.at[rows_w, :], kvp.at[rows_w, col(n, CB)],
                     agz_s.at[d], agz_r.at[d], (w, node_at(d))) for d in range(1, N)}
    near = [d for d in (1, N - 1) if 0 < d < N]
    order = list(dict.fromkeys(near + list(range(1, N))))
    for d in order:
        agz[d].start()
    nxs = [remote(normed.at[:, col(p * 2 + 1 - core, SN)], nx.at[p, 1], nxs_s.at[p], nxs_r.at[p], sib)
           for p in range(PC)]
    for x in nxs:
        x.start()

    inv_root = HD ** (-0.5)
    c2 = inv_root * math.log2(math.e)
    TB = T // 2
    out_copies = []

    def attention(k):
        for x in head_loads[k]:
            x.wait()
        kc = pl.ds(k * HD, HD)
        kt_v[...] = k_v[:, kc].astype(F32).T.astype(BF16)
        dk_v[...] = jnp.zeros_like(dk_v)
        dv_v[...] = jnp.zeros_like(dv_v)

        def head(g, carry):
            hc = col(k * GROUP + g, HD)
            q = q_v[:, hc]
            do = g_v[:, hc]
            scores, probs = [], []
            for j in range(2):
                L = (j + 1) * TB
                tr = slice(j * TB, (j + 1) * TB)
                s = dot(k_v[:L, kc], q[tr], 1, 1)
                dp = dot(v_v[:L, kc], do[tr], 1, 1)
                si = lax.broadcasted_iota(jnp.int32, (TB, TB), 0)
                ti = lax.broadcasted_iota(jnp.int32, (TB, TB), 1)
                last = jnp.where(si <= ti, s[L - TB:], -jnp.inf)
                s = jnp.concatenate([s[:L - TB], last], axis=0) if j else last
                m = jnp.max(s, axis=0, keepdims=True)
                e = jnp.exp2((s - m) * c2)
                p = e * (1.0 / jnp.sum(e, axis=0, keepdims=True))
                delta = jnp.sum(p * dp, axis=0, keepdims=True)
                ds = (p * (dp - delta)).astype(BF16)
                dq = dot(kt_v[:, :L], ds, 1, 0) * inv_root
                qg_v[pl.ds(j * TB, TB), hc] = dq.T.astype(BF16)
                scores.append(ds)
                probs.append(p.astype(BF16))
            for low, x, acc in ((scores, q, dk_v), (probs, do, dv_v)):
                acc[:TB, :] += dot(jnp.concatenate([low[0], low[1][:TB]], axis=1), x, 1, 0)
                acc[TB:, :] += dot(low[1][TB:], x[TB:], 1, 0)
            return carry

        lax.fori_loop(0, GROUP, head, 0, unroll=2)
        kg = dk_v[...] * inv_root
        ku = kg * cos_v[...] + pltpu.roll(kg, HD // 2, 1) * sin_v[...]
        vg = dv_v[...]
        kvg[:, pl.ds(k * HD, HD)] = ku.astype(BF16)
        kvg[:, pl.ds(KC + k * HD, HD)] = vg.astype(BF16)
        kvt[k, 0, :HD, :] = ku.T.astype(BF16)
        kvt[k, 0, HD:, :] = vg.T.astype(BF16)
        c = pl.ds(k * HB, HB)
        oc = pltpu.make_async_copy(qg_v.at[:, c], query_out.at[:, c], out_sem.at[k])
        oc.start()
        out_copies.append(oc)
        x = remote(kvt.at[k, 0], kvt.at[k, 1], kvs_s.at[k], kvs_r.at[k], sib)
        x.start()
        return x

    sizes = ((B, A), (A, B))

    def offsets(h, d1, d2):
        return (d2, d1) if h == 0 else (d1, d2)

    def weight_part(k, kv_copy):
        kv_copy.wait_recv()
        copies = [[], []]

        def terms(h, d1):
            s2 = sizes[h][1]
            for d2 in range(s2):
                p = chip_at(*offsets(h, d1, d2))
                lanes = pl.ds(h * SH, SH)
                term = dot(kvt[k, 0], nx[p, 0, :, lanes], 1, 0) + dot(kvt[k, 1], nx[p, 1, :, lanes], 1, 0)
                wsend[k, h, d1 * s2 + d2] = (term * grad_scale).astype(BF16)
            if d1:
                x = remote(wsend.at[k, h, pl.ds(d1 * s2, s2)], wrecv.at[k, h, pl.ds((d1 - 1) * s2, s2)],
                           p1_s.at[k, h, d1], p1_r.at[k, h, d1], plane(*offsets(h, d1, 0)))
                x.start()
                copies[h].append(x)

        for d1 in range(1, max(A, B)):
            for h in range(2):
                if d1 < sizes[h][0]:
                    terms(h, d1)
        for h in range(2):
            terms(h, 0)
        return copies

    def first_total(k, h, d2):
        s1, s2 = sizes[h]
        total = wsend[k, h, d2].astype(F32)
        for d1 in range(1, s1):
            total += wrecv[k, h, (d1 - 1) * s2 + d2].astype(F32)
        return total

    def plane_first(k, copies):
        sends = [[], []]
        for h in range(2):
            for x in copies[h]:
                x.wait_recv()
            for d2 in range(1, sizes[h][1]):
                fsend[k, h, d2 - 1] = first_total(k, h, d2).astype(BF16)
                x = remote(fsend.at[k, h, d2 - 1], frecv.at[k, h, d2 - 1], p2_s.at[k, h, d2], p2_r.at[k, h, d2],
                           plane(*offsets(h, 0, d2)))
                x.start()
                sends[h].append(x)
        return sends

    def plane_second(k, copies):
        for h in range(2):
            total = first_total(k, h, 0)
            for x in copies[h]:
                x.wait_recv()
            for d2 in range(1, sizes[h][1]):
                total += frecv[k, h, d2 - 1].astype(F32)
            nbuf[k, pl.ds(h * SH, SH), :] = total.T.astype(BF16)
        sends = []
        for d in range(1, N):
            x = remote(nbuf.at[k, col(node_at(d), R), :], nrecv.at[k, d - 1], nd_s.at[k, d], nd_r.at[k, d],
                       (w, node_at(d)))
            x.start()
            sends.append(x)
        return sends

    def final_sum(k, copies):
        for x in copies:
            x.wait_recv()
        total = nbuf[k, col(n, R), :].astype(F32)
        for d in range(1, N):
            total += nrecv[k, d - 1].astype(F32)
        wo_v[:, pl.ds(k * HD, HD)] = total[:, :HD]
        wo_v[:, pl.ds(KC + k * HD, HD)] = total[:, HD:]

    RH = RW // 2

    def piece(d, da, db, half=None):
        first = (chip_at(A - da, B - db) * 2 + core) * RW
        rows = pl.ds(pl.multiple_of(first, RW), RW)
        if half is not None:
            rows = pl.ds(pl.multiple_of(first + half * RH, RH), RH)
        return kvp.at[rows, col(node_at(N - d), CB)]

    gathers = []

    def push(ref, s, r, dev):
        x = remote(ref, ref, s, r, dev)
        x.start()
        gathers.append(x)
        return x

    got = {}

    def gather_plane(d):
        agz[d].wait_recv()
        blk = piece(d, 0, 0)
        for db in range(1, B):
            got[d, 0, db] = [push(blk, agp_s.at[d, db], agp_r.at[d, db], plane(0, db))]
        for da in range(1, A):
            got[d, da, 0] = [push(blk, agp_s.at[d, da * B], agp_r.at[d, da * B], plane(da, 0))]
        got[d, 0, 0] = []
        to_sibling(d, 0, 0)

    def to_sibling(d, da, db):
        for x in got[d, da, db]:
            x.wait_recv()
        sibs[d, da, db] = push(piece(d, da, db), ags_s.at[d, da * B + db], ags_r.at[d, da * B + db], sib)

    sibs = {}

    def gather_forward(d):
        for da in range(1, A):
            for db in range(1, B):
                got[d, da, db] = []
        for db in range(1, B):
            to_sibling(d, 0, db)
            for da in range(1, A):
                i = da * B + db
                got[d, da, db].append(push(piece(d, 0, db, 0), agf_s.at[d, 0, i], agf_r.at[d, 0, i], plane(da, 0)))
        for da in range(1, A):
            to_sibling(d, da, 0)
            for db in range(1, B):
                i = da * B + db
                got[d, da, db].append(push(piece(d, da, 0, 1), agf_s.at[d, 1, i], agf_r.at[d, 1, i], plane(0, db)))

    def gather_last(d):
        for da in range(1, A):
            for db in range(1, B):
                to_sibling(d, da, db)

    for x in loads:
        x.wait()
    steps = [order[:1], order[1:2], order[2:]]

    def each(fn, i):
        for d in steps[i]:
            fn(d)

    input_rows = []

    def input_piece(da, db):
        for d in range(1, N):
            sibs[d, da, db].wait_recv()
        i = len(input_rows)
        first = chip_at(A - da, B - db) * 2
        input_rows.append(first)

        def one(c, carry):
            oc = col(first + c, RW)
            ig_v[:, oc] = dot(kvg[...], kvp[oc, :], 1, 1).astype(BF16)
            pltpu.make_async_copy(ig_v.at[:, oc], input_out.at[:, oc], ig_sem.at[i * 2 + c]).start()
            return carry

        lax.fori_loop(0, 2, one, 0)

    kvc = [attention(0)]
    each(gather_plane, 0)
    for p in range(PC):
        nx_loads[p].wait()
        nxs[p].wait_recv()
    wc = [weight_part(0, kvc[0])]
    kvc.append(attention(1))
    each(gather_plane, 1)
    each(gather_forward, 0)
    wc.append(weight_part(1, kvc[1]))
    fc = [plane_first(0, wc[0])]
    kvc.append(attention(2))
    each(gather_forward, 1)
    wc.append(weight_part(2, kvc[2]))
    fc.append(plane_first(1, wc[1]))
    nc = [plane_second(0, fc[0])]
    each(gather_last, 0)
    kvc.append(attention(3))
    wc.append(weight_part(3, kvc[3]))
    fc.append(plane_first(2, wc[2]))
    each(gather_plane, 2)
    nc.append(plane_second(1, fc[1]))
    each(gather_last, 1)
    fc.append(plane_first(3, wc[3]))
    each(gather_forward, 2)
    own.wait()
    input_piece(0, 0)
    nc.append(plane_second(2, fc[2]))
    for db in range(1, B):
        input_piece(0, db)
    nc.append(plane_second(3, fc[3]))
    for da in range(1, A):
        input_piece(da, 0)
    for k in range(KVH - 1):
        final_sum(k, nc[k])
    each(gather_last, 2)
    for da in range(1, A):
        for db in range(1, B):
            input_piece(da, db)
    final_sum(KVH - 1, nc[KVH - 1])
    wcopy = pltpu.make_async_copy(wo_v, weight_out, out_sem.at[KVH])
    wcopy.start()

    for x in list(agz.values()) + nxs + kvc + gathers:
        x.wait_send()
    for halves in wc + fc:
        for x in halves[0] + halves[1]:
            x.wait_send()
    for group in nc:
        for x in group:
            x.wait_send()
    for x in out_copies:
        x.wait()
    for i, first in enumerate(input_rows):
        for c in range(2):
            oc = col(first + c, RW)
            pltpu.make_async_copy(ig_v.at[:, oc], input_out.at[:, oc], ig_sem.at[i * 2 + c]).wait()
    wcopy.wait()


def local(normed, queries, keys, values, attn_grad, kv_proj):
    T, D = normed.shape
    W = lax.axis_size("wide")
    N = lax.axis_size("node")
    C = 2 * KVH * HD
    CB = kv_proj.shape[1]
    PC = W // 2
    R = D // (W * N)
    SN = N * R
    far = max(plane_shape(W))
    cosine, sine = rope_tables(T, HD)
    grad_scale = (T * W * N) ** (-0.5)
    dma = pltpu.SemaphoreType.DMA
    any_spec = pl.BlockSpec(memory_space=pl.ANY)
    flops = 2 * T * (HQ * 5 * T * HD + 3 * D * C)
    return pl.pallas_call(
        functools.partial(kernel, W, N, grad_scale),
        out_shape=(
            jax.ShapeDtypeStruct((T, HQ * HD), BF16),
            jax.ShapeDtypeStruct((T, D), BF16),
            jax.ShapeDtypeStruct((R, C), F32),
        ),
        in_specs=[any_spec] * 8,
        out_specs=(any_spec,) * 3,
        scratch_shapes=[
            pltpu.VMEM((T, HQ * HD), BF16),
            pltpu.VMEM((T, HQ * HD), BF16),
            pltpu.VMEM((T, KVH * HD), BF16),
            pltpu.VMEM((T, KVH * HD), BF16),
            pltpu.VMEM((T, HD), F32),
            pltpu.VMEM((T, HD), F32),
            pltpu.VMEM((HD, T), BF16),
            pltpu.VMEM((T, HD), F32),
            pltpu.VMEM((T, HD), F32),
            pltpu.VMEM((T, HQ * HD), BF16),
            pltpu.VMEM((PC, 2, T, SN), BF16),
            pltpu.VMEM((KVH, 2, 2 * HD, T), BF16),
            pltpu.VMEM((T, C), BF16),
            pltpu.VMEM((D, C), BF16),
            pltpu.VMEM((KVH, 2, PC, 2 * HD, SN // 2), BF16),
            pltpu.VMEM((KVH, 2, PC, 2 * HD, SN // 2), BF16),
            pltpu.VMEM((KVH, 2, far, 2 * HD, SN // 2), BF16),
            pltpu.VMEM((KVH, 2, far, 2 * HD, SN // 2), BF16),
            pltpu.VMEM((KVH, SN, 2 * HD), BF16),
            pltpu.VMEM((KVH, N - 1, R, 2 * HD), BF16),
            pltpu.VMEM((T, D), BF16),
            pltpu.VMEM((R, C), F32),
            dma((2, KVH)), dma((4,)), dma((PC,)), dma, dma((KVH + 1,)), dma((W,)),
            dma((PC,)), dma((PC,)), dma((KVH,)), dma((KVH,)),
            dma((KVH, 2, far)), dma((KVH, 2, far)), dma((KVH, 2, far)), dma((KVH, 2, far)),
            dma((KVH, N)), dma((KVH, N)),
            dma((N,)), dma((N,)), dma((N, PC)), dma((N, PC)),
            dma((N, 2, PC)), dma((N, 2, PC)), dma((N, PC)), dma((N, PC)),
        ],
        compiler_params=pltpu.CompilerParams(
            collective_id=0, has_side_effects=True, vmem_limit_bytes=60 * 1024 * 1024),
        cost_estimate=pl.CostEstimate(flops=flops, bytes_accessed=24 * T * D, transcendentals=HQ * T * T),
    )(normed, queries, keys, values, attn_grad, kv_proj, cosine, sine)


def solution(mesh):
    rows = P(("wide", "node"), None)
    return jax.shard_map(
        local,
        mesh=mesh,
        in_specs=(rows, rows, rows, rows, rows, P(None, "node")),
        out_specs=(rows, rows, rows),
        check_vma=False,
    )
```

```python
import functools
import math

import jax
import jax.numpy as jnp
import numpy as np
from jax import lax
from jax.experimental import pallas as pl
from jax.experimental.pallas import tpu as pltpu
from jax.sharding import PartitionSpec as P

HQ = 16
KVH = 4
HD = 128
GROUP = HQ // KVH
ROPE_BASE = 500000.0
MESH = pl.DeviceIdType.MESH
F32 = jnp.float32
BF16 = jnp.bfloat16


def rope_tables(length, size):
    half_size = size // 2
    frequency = np.power(
        np.float32(ROPE_BASE), -np.arange(half_size, dtype=np.float32) * np.float32(2.0 / size)
    ).astype(np.float32)
    angles = np.arange(length, dtype=np.float32)[:, None] * frequency[None, :]
    cosine = np.cos(angles.astype(np.float64))
    sine = np.sin(angles.astype(np.float64))
    return (
        jnp.asarray(np.concatenate([cosine, cosine], axis=1), F32),
        jnp.asarray(np.concatenate([sine, -sine], axis=1), F32),
    )


def dot(a, b, ca, cb):
    return lax.dot_general(a, b, (((ca,), (cb,)), ((), ())), preferred_element_type=F32)


def plane_shape(W):
    chips = W // 2
    rows = 2 if chips % 2 == 0 else 1
    return rows, chips // rows


def kernel(W, N, grad_scale, normed, queries, keys, values, attn_grad, kv_proj, cosine, sine,
           query_out, input_out, weight_out,
           q_v, g_v, k_v, v_v, cos_v, sin_v, kt_v, dk_v, dv_v, qg_v, nx, kvt, kvg, kvp,
           wsend, wrecv, fsend, frecv, nbuf, nrecv, ig_v, wo_v,
           qg_sem, kv_sem, nx_sem, own_sem, out_sem, ig_sem,
           nxs_s, nxs_r, kvs_s, kvs_r, p1_s, p1_r, p2_s, p2_r, nd_s, nd_r,
           agz_s, agz_r, agp_s, agp_r, agf_s, agf_r, ags_s, ags_r):
    T, D = normed.shape
    KC = KVH * HD
    CB = kv_proj.shape[1]
    PC = W // 2
    R = D // (W * N)
    SN = N * R
    SH = SN // 2
    RW = D // W
    A, B = plane_shape(W)
    HB = GROUP * HD
    w = lax.axis_index("wide")
    n = lax.axis_index("node")
    core = lax.rem(w, 2)
    chip = lax.div(w, 2)
    sib = (chip * 2 + (1 - core), n)

    ca, cb = lax.div(chip, B), lax.rem(chip, B)

    def chip_at(da, db):
        return lax.rem(ca + da, A) * B + lax.rem(cb + db, B)

    def node_at(d):
        return lax.rem(n + d, N)

    def plane(da, db):
        return (chip_at(da, db) * 2 + core, n)

    def col(i, size):
        return pl.ds(pl.multiple_of(i * size, size), size)

    def remote(src, dst, s, r, dev):
        return pltpu.make_async_remote_copy(
            src_ref=src, dst_ref=dst, send_sem=s, recv_sem=r, device_id=dev, device_id_type=MESH)

    loads = [pltpu.make_async_copy(a, b, kv_sem.at[i]) for i, (a, b) in enumerate(
        ((keys, k_v), (values, v_v), (cosine, cos_v), (sine, sin_v)))]
    head_loads = []
    for k in range(KVH):
        c = pl.ds(k * HB, HB)
        head_loads.append((
            pltpu.make_async_copy(queries.at[:, c], q_v.at[:, c], qg_sem.at[0, k]),
            pltpu.make_async_copy(attn_grad.at[:, c], g_v.at[:, c], qg_sem.at[1, k])))
    for x in loads[:2] + list(head_loads[0]) + loads[2:]:
        x.start()
    for k in range(1, KVH):
        for x in head_loads[k]:
            x.start()
    nx_loads = [pltpu.make_async_copy(normed.at[:, col(p * 2 + core, SN)], nx.at[p, 0], nx_sem.at[p])
                for p in range(PC)]
    own = pltpu.make_async_copy(kv_proj, kvp.at[n], own_sem)

    barrier = pltpu.get_barrier_semaphore()
    partners = [sib] + [plane(d, 0) for d in range(1, A)] + [plane(0, d) for d in range(1, B)] + [(w, node_at(d)) for d in range(1, N)]
    for dev in partners:
        pl.semaphore_signal(barrier, inc=1, device_id=dev, device_id_type=MESH)
    for x in nx_loads:
        x.start()
    own.start()
    pl.semaphore_wait(barrier, len(partners))

    rows_w = col(w, RW)
    agz = {d: remote(kv_proj.at[rows_w, :], kvp.at[n, rows_w, :],
                     agz_s.at[d], agz_r.at[d], (w, node_at(d))) for d in range(1, N)}
    near = [d for d in (1, N - 1) if 0 < d < N]
    order = list(dict.fromkeys(near + list(range(1, N))))
    for d in order:
        agz[d].start()
    nxs = [remote(normed.at[:, col(p * 2 + 1 - core, SN)], nx.at[p, 1], nxs_s.at[p], nxs_r.at[p], sib)
           for p in range(PC)]
    for x in nxs:
        x.start()

    inv_root = HD ** (-0.5)
    c2 = inv_root * math.log2(math.e)
    TB = T // 2
    out_copies = []

    def attention(k):
        for x in head_loads[k]:
            x.wait()
        kc = pl.ds(k * HD, HD)
        kt_v[...] = k_v[:, kc].astype(F32).T.astype(BF16)
        dk_v[...] = jnp.zeros_like(dk_v)
        dv_v[...] = jnp.zeros_like(dv_v)

        def head(g, carry):
            hc = col(k * GROUP + g, HD)
            q = q_v[:, hc]
            do = g_v[:, hc]
            scores, probs = [], []
            for j in range(2):
                L = (j + 1) * TB
                tr = slice(j * TB, (j + 1) * TB)
                s = dot(k_v[:L, kc], q[tr], 1, 1)
                dp = dot(v_v[:L, kc], do[tr], 1, 1)
                si = lax.broadcasted_iota(jnp.int32, (TB, TB), 0)
                ti = lax.broadcasted_iota(jnp.int32, (TB, TB), 1)
                last = jnp.where(si <= ti, s[L - TB:], -jnp.inf)
                s = jnp.concatenate([s[:L - TB], last], axis=0) if j else last
                m = jnp.max(s, axis=0, keepdims=True)
                e = jnp.exp2((s - m) * c2)
                p = e * (1.0 / jnp.sum(e, axis=0, keepdims=True))
                delta = jnp.sum(p * dp, axis=0, keepdims=True)
                ds = (p * (dp - delta)).astype(BF16)
                dq = dot(kt_v[:, :L], ds, 1, 0) * inv_root
                qg_v[pl.ds(j * TB, TB), hc] = dq.T.astype(BF16)
                scores.append(ds)
                probs.append(p.astype(BF16))
            for low, x, acc in ((scores, q, dk_v), (probs, do, dv_v)):
                acc[:TB, :] += dot(jnp.concatenate([low[0], low[1][:TB]], axis=1), x, 1, 0)
                acc[TB:, :] += dot(low[1][TB:], x[TB:], 1, 0)
            return carry

        lax.fori_loop(0, GROUP, head, 0, unroll=2)
        kg = dk_v[...] * inv_root
        ku = kg * cos_v[...] + pltpu.roll(kg, HD // 2, 1) * sin_v[...]
        vg = dv_v[...]
        kvg[:, pl.ds(k * HD, HD)] = ku.astype(BF16)
        kvg[:, pl.ds(KC + k * HD, HD)] = vg.astype(BF16)
        kvt[k, 0, :HD, :] = ku.T.astype(BF16)
        kvt[k, 0, HD:, :] = vg.T.astype(BF16)
        c = pl.ds(k * HB, HB)
        oc = pltpu.make_async_copy(qg_v.at[:, c], query_out.at[:, c], out_sem.at[k])
        oc.start()
        out_copies.append(oc)
        x = remote(kvt.at[k, 0], kvt.at[k, 1], kvs_s.at[k], kvs_r.at[k], sib)
        x.start()
        return x

    sizes = ((B, A), (A, B))

    def offsets(h, d1, d2):
        return (d2, d1) if h == 0 else (d1, d2)

    def weight_part(k, kv_copy):
        kv_copy.wait_recv()
        copies = [[], []]

        def terms(h, d1):
            s2 = sizes[h][1]
            for d2 in range(s2):
                p = chip_at(*offsets(h, d1, d2))
                lanes = pl.ds(h * SH, SH)
                term = dot(kvt[k, 0], nx[p, 0, :, lanes], 1, 0) + dot(kvt[k, 1], nx[p, 1, :, lanes], 1, 0)
                wsend[k, h, d1 * s2 + d2] = (term * grad_scale).astype(BF16)
            if d1:
                x = remote(wsend.at[k, h, pl.ds(d1 * s2, s2)], wrecv.at[k, h, pl.ds((d1 - 1) * s2, s2)],
                           p1_s.at[k, h, d1], p1_r.at[k, h, d1], plane(*offsets(h, d1, 0)))
                x.start()
                copies[h].append(x)

        for d1 in range(1, max(A, B)):
            for h in range(2):
                if d1 < sizes[h][0]:
                    terms(h, d1)
        for h in range(2):
            terms(h, 0)
        return copies

    def first_total(k, h, d2):
        s1, s2 = sizes[h]
        total = wsend[k, h, d2].astype(F32)
        for d1 in range(1, s1):
            total += wrecv[k, h, (d1 - 1) * s2 + d2].astype(F32)
        return total

    def plane_first(k, copies):
        sends = [[], []]
        for h in range(2):
            for x in copies[h]:
                x.wait_recv()
            for d2 in range(1, sizes[h][1]):
                fsend[k, h, d2 - 1] = first_total(k, h, d2).astype(BF16)
                x = remote(fsend.at[k, h, d2 - 1], frecv.at[k, h, d2 - 1], p2_s.at[k, h, d2], p2_r.at[k, h, d2],
                           plane(*offsets(h, 0, d2)))
                x.start()
                sends[h].append(x)
        return sends

    def plane_second(k, copies):
        for h in range(2):
            total = first_total(k, h, 0)
            for x in copies[h]:
                x.wait_recv()
            for d2 in range(1, sizes[h][1]):
                total += frecv[k, h, d2 - 1].astype(F32)
            nbuf[k, pl.ds(h * SH, SH), :] = total.T.astype(BF16)
        sends = []
        for d in range(1, N):
            x = remote(nbuf.at[k, col(node_at(d), R), :], nrecv.at[k, d - 1], nd_s.at[k, d], nd_r.at[k, d],
                       (w, node_at(d)))
            x.start()
            sends.append(x)
        return sends

    def final_sum(k, copies):
        for x in copies:
            x.wait_recv()
        total = nbuf[k, col(n, R), :].astype(F32)
        for d in range(1, N):
            total += nrecv[k, d - 1].astype(F32)
        wo_v[:, pl.ds(k * HD, HD)] = total[:, :HD]
        wo_v[:, pl.ds(KC + k * HD, HD)] = total[:, HD:]

    RH = RW // 2

    def piece(d, da, db, half=None):
        first = (chip_at(A - da, B - db) * 2 + core) * RW
        rows = pl.ds(pl.multiple_of(first, RW), RW)
        if half is not None:
            rows = pl.ds(pl.multiple_of(first + half * RH, RH), RH)
        return kvp.at[node_at(N - d), rows, :]

    gathers = []

    def push(ref, s, r, dev):
        x = remote(ref, ref, s, r, dev)
        x.start()
        gathers.append(x)
        return x

    got = {}

    def gather_plane(d):
        agz[d].wait_recv()
        blk = piece(d, 0, 0)
        for db in range(1, B):
            got[d, 0, db] = [push(blk, agp_s.at[d, db], agp_r.at[d, db], plane(0, db))]
        for da in range(1, A):
            got[d, da, 0] = [push(blk, agp_s.at[d, da * B], agp_r.at[d, da * B], plane(da, 0))]
        got[d, 0, 0] = []
        to_sibling(d, 0, 0)

    def to_sibling(d, da, db):
        for x in got[d, da, db]:
            x.wait_recv()
        sibs[d, da, db] = push(piece(d, da, db), ags_s.at[d, da * B + db], ags_r.at[d, da * B + db], sib)

    sibs = {}

    def gather_forward(d):
        for da in range(1, A):
            for db in range(1, B):
                got[d, da, db] = []
        for db in range(1, B):
            to_sibling(d, 0, db)
            for da in range(1, A):
                i = da * B + db
                got[d, da, db].append(push(piece(d, 0, db, 0), agf_s.at[d, 0, i], agf_r.at[d, 0, i], plane(da, 0)))
        for da in range(1, A):
            to_sibling(d, da, 0)
            for db in range(1, B):
                i = da * B + db
                got[d, da, db].append(push(piece(d, da, 0, 1), agf_s.at[d, 1, i], agf_r.at[d, 1, i], plane(0, db)))

    def gather_last(d):
        for da in range(1, A):
            for db in range(1, B):
                to_sibling(d, da, db)

    for x in loads:
        x.wait()
    steps = [order[:1], order[1:2], order[2:]]

    def each(fn, i):
        for d in steps[i]:
            fn(d)

    input_rows = []

    def input_piece(da, db):
        for d in range(1, N):
            sibs[d, da, db].wait_recv()
        i = len(input_rows)
        first = chip_at(A - da, B - db) * 2
        input_rows.append(first)

        def one(c, carry):
            oc = col(first + c, RW)
            weights = jnp.concatenate([kvp[j, oc, :] for j in range(N)], axis=1)
            ig_v[:, oc] = dot(kvg[...], weights, 1, 1).astype(BF16)
            pltpu.make_async_copy(ig_v.at[:, oc], input_out.at[:, oc], ig_sem.at[i * 2 + c]).start()
            return carry

        lax.fori_loop(0, 2, one, 0)

    kvc = [attention(0)]
    each(gather_plane, 0)
    for p in range(PC):
        nx_loads[p].wait()
        nxs[p].wait_recv()
    wc = [weight_part(0, kvc[0])]
    kvc.append(attention(1))
    each(gather_plane, 1)
    each(gather_forward, 0)
    wc.append(weight_part(1, kvc[1]))
    fc = [plane_first(0, wc[0])]
    kvc.append(attention(2))
    each(gather_forward, 1)
    wc.append(weight_part(2, kvc[2]))
    fc.append(plane_first(1, wc[1]))
    nc = [plane_second(0, fc[0])]
    each(gather_last, 0)
    kvc.append(attention(3))
    wc.append(weight_part(3, kvc[3]))
    fc.append(plane_first(2, wc[2]))
    each(gather_plane, 2)
    nc.append(plane_second(1, fc[1]))
    each(gather_last, 1)
    fc.append(plane_first(3, wc[3]))
    each(gather_forward, 2)
    own.wait()
    input_piece(0, 0)
    nc.append(plane_second(2, fc[2]))
    for db in range(1, B):
        input_piece(0, db)
    nc.append(plane_second(3, fc[3]))
    for da in range(1, A):
        input_piece(da, 0)
    for k in range(KVH - 1):
        final_sum(k, nc[k])
    each(gather_last, 2)
    for da in range(1, A):
        for db in range(1, B):
            input_piece(da, db)
    final_sum(KVH - 1, nc[KVH - 1])
    wcopy = pltpu.make_async_copy(wo_v, weight_out, out_sem.at[KVH])
    wcopy.start()

    for x in list(agz.values()) + nxs + kvc + gathers:
        x.wait_send()
    for halves in wc + fc:
        for x in halves[0] + halves[1]:
            x.wait_send()
    for group in nc:
        for x in group:
            x.wait_send()
    for x in out_copies:
        x.wait()
    for i, first in enumerate(input_rows):
        for c in range(2):
            oc = col(first + c, RW)
            pltpu.make_async_copy(ig_v.at[:, oc], input_out.at[:, oc], ig_sem.at[i * 2 + c]).wait()
    wcopy.wait()


def local(normed, queries, keys, values, attn_grad, kv_proj):
    T, D = normed.shape
    W = lax.axis_size("wide")
    N = lax.axis_size("node")
    C = 2 * KVH * HD
    CB = kv_proj.shape[1]
    PC = W // 2
    R = D // (W * N)
    SN = N * R
    far = max(plane_shape(W))
    cosine, sine = rope_tables(T, HD)
    grad_scale = (T * W * N) ** (-0.5)
    dma = pltpu.SemaphoreType.DMA
    any_spec = pl.BlockSpec(memory_space=pl.ANY)
    flops = 2 * T * (HQ * 5 * T * HD + 3 * D * C)
    return pl.pallas_call(
        functools.partial(kernel, W, N, grad_scale),
        out_shape=(
            jax.ShapeDtypeStruct((T, HQ * HD), BF16),
            jax.ShapeDtypeStruct((T, D), BF16),
            jax.ShapeDtypeStruct((R, C), F32),
        ),
        in_specs=[any_spec] * 8,
        out_specs=(any_spec,) * 3,
        scratch_shapes=[
            pltpu.VMEM((T, HQ * HD), BF16),
            pltpu.VMEM((T, HQ * HD), BF16),
            pltpu.VMEM((T, KVH * HD), BF16),
            pltpu.VMEM((T, KVH * HD), BF16),
            pltpu.VMEM((T, HD), F32),
            pltpu.VMEM((T, HD), F32),
            pltpu.VMEM((HD, T), BF16),
            pltpu.VMEM((T, HD), F32),
            pltpu.VMEM((T, HD), F32),
            pltpu.VMEM((T, HQ * HD), BF16),
            pltpu.VMEM((PC, 2, T, SN), BF16),
            pltpu.VMEM((KVH, 2, 2 * HD, T), BF16),
            pltpu.VMEM((T, C), BF16),
            pltpu.VMEM((N, D, CB), BF16),
            pltpu.VMEM((KVH, 2, PC, 2 * HD, SN // 2), BF16),
            pltpu.VMEM((KVH, 2, PC, 2 * HD, SN // 2), BF16),
            pltpu.VMEM((KVH, 2, far, 2 * HD, SN // 2), BF16),
            pltpu.VMEM((KVH, 2, far, 2 * HD, SN // 2), BF16),
            pltpu.VMEM((KVH, SN, 2 * HD), BF16),
            pltpu.VMEM((KVH, N - 1, R, 2 * HD), BF16),
            pltpu.VMEM((T, D), BF16),
            pltpu.VMEM((R, C), F32),
            dma((2, KVH)), dma((4,)), dma((PC,)), dma, dma((KVH + 1,)), dma((W,)),
            dma((PC,)), dma((PC,)), dma((KVH,)), dma((KVH,)),
            dma((KVH, 2, far)), dma((KVH, 2, far)), dma((KVH, 2, far)), dma((KVH, 2, far)),
            dma((KVH, N)), dma((KVH, N)),
            dma((N,)), dma((N,)), dma((N, PC)), dma((N, PC)),
            dma((N, 2, PC)), dma((N, 2, PC)), dma((N, PC)), dma((N, PC)),
        ],
        compiler_params=pltpu.CompilerParams(
            collective_id=0, has_side_effects=True, vmem_limit_bytes=60 * 1024 * 1024),
        cost_estimate=pl.CostEstimate(flops=flops, bytes_accessed=24 * T * D, transcendentals=HQ * T * T),
    )(normed, queries, keys, values, attn_grad, kv_proj, cosine, sine)


def solution(mesh):
    rows = P(("wide", "node"), None)
    return jax.shard_map(
        local,
        mesh=mesh,
        in_specs=(rows, rows, rows, rows, rows, P(None, "node")),
        out_specs=(rows, rows, rows),
        check_vma=False,
    )
```
